768 devices in a mesh: grid: 96 (over z_hi, x, y), depth: 8 (over z_lo, core).
Axes of the slice: x: 4, y: 8, z: 12 (z_hi: 3, z_lo: 4; z = z_hi * 4 + z_lo), core: 2. Of those that a mesh axis runs over, the one named last changes fastest.
Arguments:
- density: float32 [384, 8, 32, 32], P('grid', 'depth'), may hold values from -1 to 1
- columns: int32 [384, 8, 1], P('grid', 'depth'), may hold values from 0 to 47, as said below
- fill_columns: int32 [384, 8, 4], P('grid', 'depth'), may hold values from 0 to 47, as said below
Outputs:
- purified: float32 [384, 8, 32, 128], P('grid', 'depth')
The draws below stay inside these ranges and needn't reach their ends.
Inputs may be any that keep to these rules, and one draw needn't show every extreme that they name: `columns`: the 1 entries of one block row and one column group are distinct. `fill_columns`: the 4 entries of one block row and one column group are distinct.
All inputs are finite; a program needn't handle non-finite values.
Results may differ from the reference program's by a relative error of at most 0.0003.
Values sent between devices are 32-bit elements; how exact they have to be, the bound alone decides.
No kernel may reach another device: no remote copies, remote signals or barrier semaphores. Data moves between devices by JAX's collectives and lax.ppermute only.
A program may use at most 32 MiB of HBM per device.

```python
import jax
import jax.numpy as jnp
from jax import lax

BS = 32
KS = 1
KF = 4
LB = 8
NB = 384
NCG = 8
CB = 48


def label_tables(key):
    keys = jax.random.split(jax.random.fold_in(key, 5), NCG)
    orders = jax.vmap(lambda one_key: jax.random.permutation(one_key, CB))(keys).astype(jnp.int32)
    inverse = jnp.argsort(orders, axis=1, stable=True).astype(jnp.int32)
    row_label = (inverse // LB).reshape(-1)
    members = orders.reshape(NCG, CB // LB, LB)
    return (row_label, members)


def pick_members(key, row_label, members, count):
    base = jax.random.randint(key, (NB, NCG, 1), 0, LB)
    positions = (base + jnp.arange(count, dtype=jnp.int32)[None, None, :]) % LB
    group_index = jnp.arange(NCG, dtype=jnp.int32)[None, :, None]
    label_index = row_label[:, None, None]
    return members[group_index, label_index, positions].astype(jnp.int32)


def draw_columns(key, part):
    row_label, members = label_tables(key)
    key = jax.random.fold_in(key, 11)
    return pick_members(key, row_label, members, KS)


def draw_fill_columns(key, part):
    row_label, members = label_tables(key)
    key = jax.random.fold_in(key, 23)
    return pick_members(key, row_label, members, KF)


def shard_levels(own_key, extent, shards, least, high):
    factor_of, own = 1.0, jax.random.fold_in(own_key, 6)
    for position, parts in shards:
        steps = jnp.exp(jax.random.uniform(jax.random.fold_in(own, position), (parts,), jnp.float32, least / len(shards), high / len(shards)))
        factor_of = factor_of * jnp.repeat(steps, extent[position] // parts).reshape([-1 if axis == position else 1 for axis in range(len(extent))])
    return factor_of


def scatter_about(rng, dims, deviation, reach, cuts=(), kind=jnp.bfloat16):
    values = deviation * jax.random.normal(rng, dims, jnp.float32)
    if cuts:
        values = values * shard_levels(rng, dims, cuts, -0.22, 0.18)
    return jnp.clip(values, -reach, reach).astype(kind)


def setup_inputs(seed: int = 0) -> dict:
    streams_of = jax.random.split(jax.random.key(seed), 4)
    return {
        "density": scatter_about(streams_of[0], (NB, NCG, BS, KS * BS), BS ** -0.5, 1.0, ((0, 96), (1, 8)), jnp.float32),
        "columns": draw_columns(jax.random.fold_in(streams_of[3], 71), 0),
        "fill_columns": draw_fill_columns(jax.random.fold_in(streams_of[3], 71), 0),
    }


def as_blocks(values, block_size):
    groups, rows_here, width = values.shape
    slots = width // block_size
    shaped = values.reshape(groups, rows_here, slots, block_size)
    return shaped.transpose(0, 2, 1, 3).reshape(groups * slots, rows_here, block_size)


def multiply_row(left, left_columns, row_fill, density, columns):
    offsets = jnp.arange(NCG, dtype=jnp.int32)[:, None] * CB
    needed = (left_columns.astype(jnp.int32) + offsets).reshape(-1)
    left_blocks = as_blocks(left, BS)
    chosen = density[needed].reshape(needed.shape[0], NCG, BS, KS, BS)
    products = jnp.einsum('tab,tebsc->tesac', left_blocks, chosen, precision=lax.Precision.HIGHEST)
    landing = columns[needed]
    match = (landing[:, :, :, None] == row_fill[None, :, None, :]).astype(jnp.float32)
    result = jnp.einsum('tesf,tesac->eafc', match, products, precision=lax.Precision.HIGHEST)
    return result.reshape(NCG, BS, KF * BS)


def reference(density, columns, fill_columns):
    def one_row(row_index):
        own_fill = fill_columns[row_index]
        squared = multiply_row(density[row_index], columns[row_index], own_fill, density, columns)
        cubed = multiply_row(squared, own_fill, own_fill, density, columns)
        return 3.0 * squared - 2.0 * cubed
    return lax.map(one_row, jnp.arange(NB, dtype=jnp.int32))
```

```python
import functools

import jax
import jax.numpy as jnp
from jax import lax
from jax.experimental import pallas as pl
from jax.experimental.pallas import tpu as pltpu
from jax.sharding import Mesh, PartitionSpec as P

BS = 32
ROWS = 4
KF = 4
CB = 48
NCG = 8
LANES = 128
TILE = 40
AXES = ("zh", "x", "y", "zl", "c")
SIZES = (3, 4, 8, 4, 2)
NZ, NX, NY, NL, NC = SIZES
PIECE = NZ * NY * TILE


def place(slab, code, wanted, lane_slot):
    start = pl.multiple_of((code >> 2) * TILE, 8)
    keep = lane_slot == (code & 3)
    block = jnp.where(keep, slab[pl.ds(start, TILE), :], 0.0)
    block = block + pltpu.roll(block, 64, 1)
    block = block + pltpu.roll(block, 32, 1)
    return jnp.where(block[BS : BS + 1, :] == wanted, block[:BS, :], 0.0)


def load_slab(pieces, slab, sems):
    copies = [
        pltpu.make_async_copy(piece, slab.at[pl.ds(n * PIECE, PIECE), :], sems.at[n])
        for n, piece in enumerate(pieces)
    ]
    for copy in copies:
        copy.start()
    return copies


def square_kernel(codes, wanted, left, s0, s1, s2, s3, out, slab, right, sems):
    copies = load_slab((s0, s1, s2, s3), slab, sems)
    lane_slot = lax.broadcasted_iota(jnp.int32, (TILE, LANES), 1) // BS
    for copy in copies:
        copy.wait()
    for row in range(ROWS):
        want = wanted[row : row + 1, :]
        for t in range(NCG):
            right[t * BS : (t + 1) * BS, :] = place(slab, codes[row * NCG + t], want, lane_slot)
        out[row * BS : (row + 1) * BS, :] = jnp.dot(
            left[row], right[...], precision=lax.Precision.HIGHEST, preferred_element_type=jnp.float32
        )


def cube_kernel(codes, wanted, squares, own, s0, s1, s2, s3, out, slab, right, sems):
    copies = load_slab((s0, s1, s2, s3), slab, sems)
    lane_slot = lax.broadcasted_iota(jnp.int32, (TILE, LANES), 1) // BS
    for copy in copies:
        copy.wait()
    for row in range(ROWS):
        want = wanted[row : row + 1, :]
        rows = slice(row * BS, (row + 1) * BS)
        total = jnp.zeros((BS, LANES), jnp.float32)
        for group in range(NCG):
            for slot in range(KF):
                t = group * KF + slot
                right[t * BS : (t + 1) * BS, :] = place(slab, codes[row * NCG * KF + t], want, lane_slot)
            total = total + jnp.dot(
                squares[group % NC, group // NC, rows, :],
                right[group * LANES : (group + 1) * LANES, :],
                precision=lax.Precision.HIGHEST,
                preferred_element_type=jnp.float32,
            )
        out[rows, :] = 3.0 * own[rows, :] - 2.0 * total


def vmem():
    return pl.BlockSpec(memory_space=pltpu.VMEM)


def smem():
    return pl.BlockSpec(memory_space=pltpu.SMEM)


def anywhere():
    return pl.BlockSpec(memory_space=pl.ANY)


def square(codes, wanted, left, pieces):
    return pl.pallas_call(
        square_kernel,
        out_shape=jax.ShapeDtypeStruct((ROWS * BS, LANES), jnp.float32),
        in_specs=[smem(), vmem(), vmem()] + [anywhere()] * 4,
        out_specs=vmem(),
        scratch_shapes=[
            pltpu.VMEM((NX * PIECE, LANES), jnp.float32),
            pltpu.VMEM((NCG * BS, LANES), jnp.float32),
            pltpu.SemaphoreType.DMA((4,)),
        ],
        compiler_params=pltpu.CompilerParams(vmem_limit_bytes=16 * 2**20),
        name="square",
    )(codes, wanted, left, *pieces)


def cube(codes, wanted, squares, own, pieces):
    return pl.pallas_call(
        cube_kernel,
        out_shape=jax.ShapeDtypeStruct((ROWS * BS, LANES), jnp.float32),
        in_specs=[smem(), vmem(), vmem(), vmem()] + [anywhere()] * 4,
        out_specs=vmem(),
        scratch_shapes=[
            pltpu.VMEM((NX * PIECE, LANES), jnp.float32),
            pltpu.VMEM((NCG * KF * BS, LANES), jnp.float32),
            pltpu.SemaphoreType.DMA((4,)),
        ],
        compiler_params=pltpu.CompilerParams(vmem_limit_bytes=16 * 2**20),
        name="cube",
    )(codes, wanted, squares, own, *pieces)


def to_all(value, axes, count):
    copies = lax.optimization_barrier(jnp.broadcast_to(value[None], (count,) + value.shape))
    return lax.all_to_all(copies, axes, 0, 0)


def codes_of(block_row):
    owner = block_row // ROWS
    distance = (owner // NY % NX - lax.axis_index("x")) % NX
    return ((distance * NZ + owner // (NX * NY)) * NY + owner % NY) * ROWS + block_row % ROWS


def local(density, columns, fill_columns):
    data = density[:, 0].transpose(1, 0, 2).reshape(BS, LANES)
    numbers = jnp.concatenate([columns[:, 0, :].T, fill_columns[:, 0]]).astype(jnp.float32)
    numbers = jnp.pad(jnp.repeat(numbers, BS, axis=1), ((0, 3), (0, 0)))
    tile = jnp.concatenate([data, numbers])

    plane = to_all(tile, ("zh", "y"), NZ * NY)
    plane, tile = lax.optimization_barrier((plane, tile))
    own = plane.reshape(PIECE, LANES)
    pieces = [own] + [
        lax.ppermute(own, "x", [((n + step) % NX, n) for n in range(NX)]) for step in (1, 2, 3)
    ]

    rows = to_all(tile, ("zl", "c"), NCG)
    numbers = rows[:, BS : BS + 5, ::BS].astype(jnp.int32)
    groups = jnp.arange(NCG, dtype=jnp.int32) * CB
    first = codes_of(numbers[:, 0, :].T + groups[None, :]).reshape(-1)
    second = codes_of(numbers[:, 1:, :].transpose(1, 0, 2) + groups[None, :, None]).reshape(-1)
    left = rows[:, :BS].reshape(NCG, BS, ROWS, BS).transpose(2, 1, 0, 3).reshape(ROWS, BS, NCG * BS)
    wanted = tile[BS + 1 : BS + 1 + ROWS]

    squared = square(first, wanted, left, pieces)
    squares = lax.all_gather(to_all(squared, ("zl",), NL), "c")
    purified = cube(second, wanted, squares, squared, pieces)
    return purified.reshape(ROWS, 1, BS, LANES)


def solution(mesh):
    fine = Mesh(mesh.devices.reshape(SIZES), AXES)
    grid, depth = ("zh", "x", "y"), ("zl", "c")
    in_specs = (P(grid, depth, None, None), P(grid, depth, None), P(grid, depth, None))
    out_specs = P(grid, depth, None, None)
    return jax.shard_map(local, mesh=fine, in_specs=in_specs, out_specs=out_specs, check_vma=False)
```

```python
import jax
import jax.numpy as jnp
from jax import lax
from jax.experimental import pallas as pl
from jax.experimental.pallas import tpu as pltpu
from jax.sharding import Mesh, PartitionSpec as P

BS = 32
ROWS = 4
KF = 4
CB = 48
NCG = 8
LANES = 128
TILE = 40
AXES = ("zh", "x", "yh", "yl", "zl", "c")
SIZES = (3, 4, 4, 2, 4, 2)
NZ, NX, NYH, NYL, NL, NC = SIZES
NY = NYH * NYL
FIRST, SECOND = ("zh", "yh"), ("x", "yl")
NP, NS = NZ * NYH, NX * NYL
PIECE = NP * BS + 16
GROUP = NCG * KF * BS


def place(slab, codes, wanted):
    lane_slot = lax.broadcasted_iota(jnp.int32, (8, LANES), 1) // BS
    blocks, columns = [], []
    for code in codes:
        keep = lane_slot == (code & 3)
        block = slab[pl.ds(pl.multiple_of(code >> 14, 8), BS), :].reshape(BS // 8, 8, LANES)
        column = jnp.broadcast_to(slab[pl.ds((code >> 2) & 4095, 1), :], (8, LANES))
        blocks.append(jnp.where(keep, block, 0.0))
        columns.append(jnp.where(keep, column, 0.0)[None])
    every = jnp.concatenate(blocks + columns).reshape(-1, LANES)
    every = every + pltpu.roll(every, 64, 1)
    every = every + pltpu.roll(every, 32, 1)
    count = len(codes)
    blocks = every[: count * BS].reshape(count, BS // 8, 8, LANES)
    columns = every[count * BS :].reshape(count, 8, LANES)
    lands = columns == jnp.stack(wanted)
    return jnp.where(lands[:, None], blocks, 0.0).reshape(count * BS, LANES)


def wanted_of(tile, row):
    return jnp.broadcast_to(tile[BS + 1 + row : BS + 2 + row, :], (8, LANES))


def halves(values, axis):
    high = values.astype(jnp.bfloat16)
    low = (values - high.astype(jnp.float32)).astype(jnp.bfloat16)
    return jnp.concatenate([high, low], axis=axis)


def product(total):
    return (total[:BS, :LANES] + total[:BS, LANES:]) + (total[BS:, :LANES] + total[BS:, LANES:])


def pack_kernel(columns, fill, density, out, copies):
    lane_slot = lax.broadcasted_iota(jnp.int32, (8, LANES), 1) // BS
    line = lax.broadcasted_iota(jnp.int32, (8, LANES), 0)
    numbers = jnp.zeros((8, LANES), jnp.int32)
    for slot in range(ROWS):
        numbers = jnp.where((line == 0) & (lane_slot == slot), columns[0, slot], numbers)
    for row in range(ROWS):
        for slot in range(KF):
            numbers = jnp.where((line == row + 1) & (lane_slot == slot), fill[row, slot], numbers)
    numbers = numbers.astype(jnp.float32)
    data = jnp.concatenate([density[row] for row in range(ROWS)], axis=1)
    out[:BS, :] = data
    out[BS:, :] = numbers
    for n in range(NP):
        copies[n, :BS, :] = data
        copies[n, BS:, :] = numbers


def spread_kernel(plane, out):
    for member in range(NP):
        block = plane[member, :BS, :]
        column = plane[member, BS : BS + 1, :]
        for n in range(NS):
            out[n, member * BS : (member + 1) * BS, :] = block
            out[n, NP * BS + member : NP * BS + member + 1, :] = column
    for n in range(NS):
        out[n, NP * BS + NP :, :] = jnp.zeros((PIECE - NP * BS - NP, LANES), jnp.float32)


def square_kernel(codes, tile, left, slab, out, own, right):
    for row in range(0, ROWS, 2):
        wanted = [wanted_of(tile, row)] * NCG + [wanted_of(tile, row + 1)] * NCG
        blocks = place(slab, [codes[row * NCG + t] for t in range(2 * NCG)], wanted)
        right[row * NCG * BS : (row + 2) * NCG * BS, :] = halves(blocks, 1)
    for row in range(ROWS):
        values = right[row * NCG * BS : (row + 1) * NCG * BS, :]
        result = product(jnp.dot(halves(left[row], 0), values, preferred_element_type=jnp.float32))
        rows = slice(row * BS, (row + 1) * BS)
        own[rows, :] = result
        for n in range(NL):
            out[n, rows, :] = result


def right_kernel(codes, tile, slab, out):
    batch = 16
    for row in range(ROWS):
        wanted = [wanted_of(tile, row)] * batch
        for t in range(row * NCG * KF, (row + 1) * NCG * KF, batch):
            blocks = place(slab, [codes[t + n] for n in range(batch)], wanted)
            out[t * BS : (t + batch) * BS, :] = halves(blocks, 1)


def cube_kernel(mine, other, own, right, out):
    for row in range(ROWS):
        rows = slice(row * BS, (row + 1) * BS)
        total = jnp.zeros((2 * BS, 2 * LANES), jnp.float32)
        for near in range(NL):
            values = jnp.concatenate([mine[near, rows, :], other[near, rows, :]], axis=1)
            start = row * GROUP + near * NC * LANES
            total = total + jnp.dot(
                halves(values, 0), right[start : start + NC * LANES, :], preferred_element_type=jnp.float32
            )
        out[rows, :] = 3.0 * own[rows, :] - 2.0 * product(total)


def vmem():
    return pl.BlockSpec(memory_space=pltpu.VMEM)


def smem():
    return pl.BlockSpec(memory_space=pltpu.SMEM)


def call(kernel, name, shapes, specs, args, scratch=(), limit=16 * 2**20):
    size = 4 * sum(a.size for a in args)
    shapes = [jax.ShapeDtypeStruct(*shape) for shape in shapes]
    results = pl.pallas_call(
        kernel,
        out_shape=shapes,
        in_specs=specs,
        out_specs=[vmem() for _ in shapes],
        scratch_shapes=list(scratch),
        compiler_params=pltpu.CompilerParams(vmem_limit_bytes=limit),
        cost_estimate=pl.CostEstimate(flops=2**24, bytes_accessed=size, transcendentals=0),
        name=name,
    )(*args)
    return results if len(shapes) > 1 else results[0]


def codes_of(block_row):
    owner, slot = block_row // ROWS, block_row % ROWS
    piece = owner // NY % NX * NYL + owner % NYL
    member = owner // (NX * NY) * NYH + owner % NY // NYL
    return (piece * PIECE + member * BS) * 2**14 + (piece * PIECE + NP * BS + member) * 4 + slot


def local(density, columns, fill_columns):
    f32 = jnp.float32
    tile, copies = call(
        pack_kernel, "pack", [((TILE, LANES), f32), ((NP, TILE, LANES), f32)], [smem(), smem(), vmem()],
        (columns.reshape(1, ROWS), fill_columns.reshape(ROWS, KF), density.reshape(ROWS, BS, BS)),
        limit=60 * 2**20,
    )
    plane = lax.all_to_all(copies, FIRST, 0, 0)
    pair = lax.all_gather(tile, "c")
    plane, pair = lax.optimization_barrier((plane, pair))
    pieces = call(spread_kernel, "spread", [((NS, PIECE, LANES), f32)], [vmem()], (plane,))
    slab = lax.all_to_all(pieces, SECOND, 0, 0).reshape(NS * PIECE, LANES)

    near = [pair] + [
        lax.ppermute(pair, "zl", [(n, (n + step) % NL) for n in range(NL)]) for step in range(1, NL)
    ]
    rows = jnp.stack(near).reshape(NCG, TILE, LANES)
    numbers = rows[:, BS : BS + 5, ::BS].astype(jnp.int32)
    place_here, core = lax.axis_index("zl"), lax.axis_index("c")
    steps = jnp.arange(NCG, dtype=jnp.int32)
    groups = ((place_here - steps // NC) % NL * NC + steps % NC) * CB
    first = codes_of(numbers[:, 0, :].T + groups[None, :]).reshape(-1)
    second = codes_of(numbers[:, 1:, :].transpose(1, 0, 2) + groups[None, :, None])
    second = second.reshape(ROWS, NL, NC, KF)
    places = jnp.arange(NL, dtype=jnp.int32)
    turn = ((place_here - places[:, None]) % NL == places[None, :])[None, :, :, None, None]
    second = jnp.sum(jnp.where(turn, second[:, None], 0), axis=2)
    second = jnp.where(core == 0, second, second[:, :, ::-1]).reshape(-1)
    left = rows[:, :BS].reshape(NCG, BS, ROWS, BS).transpose(2, 1, 0, 3).reshape(ROWS, BS, NCG * BS)

    shape = (ROWS * BS, LANES)
    squared, own = call(
        square_kernel, "square", [((NL,) + shape, f32), (shape, f32)], [smem(), vmem(), vmem(), vmem()],
        (first, tile, left, slab),
        [pltpu.VMEM((ROWS * NCG * BS, 2 * LANES), jnp.bfloat16)],
    )
    right = call(
        right_kernel, "right", [((ROWS * GROUP, 2 * LANES), jnp.bfloat16)], [smem(), vmem(), vmem()],
        (second, tile, slab),
    )
    mine, right = lax.optimization_barrier((lax.all_to_all(squared, "zl", 0, 0), right))
    other = lax.ppermute(mine, "c", [(0, 1), (1, 0)])
    purified = call(cube_kernel, "cube", [(shape, f32)], [vmem()] * 4, (mine, other, own, right))
    return purified.reshape(ROWS, 1, BS, LANES)


def solution(mesh):
    fine = Mesh(mesh.devices.reshape(SIZES), AXES)
    grid, depth = ("zh", "x", "yh", "yl"), ("zl", "c")
    in_specs = (P(grid, depth, None, None), P(grid, depth, None), P(grid, depth, None))
    out_specs = P(grid, depth, None, None)
    return jax.shard_map(local, mesh=fine, in_specs=in_specs, out_specs=out_specs, check_vma=False)
```

```python
import functools

import jax
import jax.numpy as jnp
from jax import lax
from jax.experimental import pallas as pl
from jax.experimental.pallas import tpu as pltpu
from jax.sharding import Mesh, PartitionSpec as P

BS = 32
ROWS = 4
KF = 4
CB = 48
NCG = 8
LANES = 128
TILE = 40
AXES = ("zh", "x", "yh", "yl", "zl", "c")
SIZES = (3, 4, 4, 2, 4, 2)
NZ, NX, NYH, NYL, NL, NC = SIZES
NY = NYH * NYL
FIRST, SECOND = ("zh", "yh"), ("x", "yl")
NP, NS = NZ * NYH, NX * NYL
PIECE = NP * BS + 16
GROUP = NCG * KF * BS


def place(slab, codes, wanted):
    lane_slot = lax.broadcasted_iota(jnp.int32, (8, LANES), 1) // BS
    blocks, columns = [], []
    for code in codes:
        keep = lane_slot == (code & 3)
        block = slab[pl.ds(pl.multiple_of(code >> 14, 8), BS), :].reshape(BS // 8, 8, LANES)
        column = jnp.broadcast_to(slab[pl.ds((code >> 2) & 4095, 1), :], (8, LANES))
        blocks.append(jnp.where(keep, block, 0.0))
        columns.append(jnp.where(keep, column, 0.0)[None])
    every = jnp.concatenate(blocks + columns).reshape(-1, LANES)
    every = every + pltpu.roll(every, 64, 1)
    every = every + pltpu.roll(every, 32, 1)
    count = len(codes)
    blocks = every[: count * BS].reshape(count, BS // 8, 8, LANES)
    columns = every[count * BS :].reshape(count, 8, LANES)
    lands = columns == jnp.stack(wanted)
    return jnp.where(lands[:, None], blocks, 0.0).reshape(count * BS, LANES)


def wanted_of(tile, row):
    return jnp.broadcast_to(tile[BS + 1 + row : BS + 2 + row, :], (8, LANES))


def halves(values, axis):
    high = values.astype(jnp.bfloat16)
    low = (values - high.astype(jnp.float32)).astype(jnp.bfloat16)
    return jnp.concatenate([high, low], axis=axis)


def product(total):
    return (total[:BS, :LANES] + total[:BS, LANES:]) + (total[BS:, :LANES] + total[BS:, LANES:])


def pack_kernel(columns, fill, density, out, copies):
    lane_slot = lax.broadcasted_iota(jnp.int32, (8, LANES), 1) // BS
    line = lax.broadcasted_iota(jnp.int32, (8, LANES), 0)
    numbers = jnp.zeros((8, LANES), jnp.int32)
    for slot in range(ROWS):
        numbers = jnp.where((line == 0) & (lane_slot == slot), columns[0, slot], numbers)
    for row in range(ROWS):
        for slot in range(KF):
            numbers = jnp.where((line == row + 1) & (lane_slot == slot), fill[row, slot], numbers)
    numbers = numbers.astype(jnp.float32)
    data = jnp.concatenate([density[row] for row in range(ROWS)], axis=1)
    out[:BS, :] = data
    out[BS:, :] = numbers
    for n in range(NP):
        copies[n, :BS, :] = data
        copies[n, BS:, :] = numbers


def spread_kernel(plane, out):
    for member in range(NP):
        block = plane[member, :BS, :]
        column = plane[member, BS : BS + 1, :]
        for n in range(NS):
            out[n, member * BS : (member + 1) * BS, :] = block
            out[n, NP * BS + member : NP * BS + member + 1, :] = column
    for n in range(NS):
        out[n, NP * BS + NP :, :] = jnp.zeros((PIECE - NP * BS - NP, LANES), jnp.float32)


def square_kernel(codes, tile, left, slab, out, own, right):
    for row in range(0, ROWS, 2):
        wanted = [wanted_of(tile, row)] * NCG + [wanted_of(tile, row + 1)] * NCG
        blocks = place(slab, [codes[row * NCG + t] for t in range(2 * NCG)], wanted)
        right[row * NCG * BS : (row + 2) * NCG * BS, :] = halves(blocks, 1)
    for row in range(ROWS):
        values = right[row * NCG * BS : (row + 1) * NCG * BS, :]
        result = product(jnp.dot(halves(left[row], 0), values, preferred_element_type=jnp.float32))
        rows = slice(row * BS, (row + 1) * BS)
        own[rows, :] = result
        for n in range(NL):
            out[n, rows, :] = result


def right_kernel(start, codes, tile, slab, out):
    batch = 16
    for row in range(ROWS // 2):
        wanted = [wanted_of(tile, start + row)] * batch
        for t in range(row * NCG * KF, (row + 1) * NCG * KF, batch):
            blocks = place(slab, [codes[start * NCG * KF + t + n] for n in range(batch)], wanted)
            out[t * BS : (t + batch) * BS, :] = halves(blocks, 1)


def cube_kernel(mine, other, own, upper, lower, out):
    for row in range(ROWS):
        right = upper if row < ROWS // 2 else lower
        rows = slice(row * BS, (row + 1) * BS)
        total = jnp.zeros((2 * BS, 2 * LANES), jnp.float32)
        for near in range(NL):
            values = jnp.concatenate([mine[near, rows, :], other[near, rows, :]], axis=1)
            start = row % (ROWS // 2) * GROUP + near * NC * LANES
            total = total + jnp.dot(
                halves(values, 0), right[start : start + NC * LANES, :], preferred_element_type=jnp.float32
            )
        out[rows, :] = 3.0 * own[rows, :] - 2.0 * product(total)


def vmem():
    return pl.BlockSpec(memory_space=pltpu.VMEM)


def smem():
    return pl.BlockSpec(memory_space=pltpu.SMEM)


def call(kernel, name, shapes, specs, args, scratch=(), limit=16 * 2**20):
    size = 4 * sum(a.size for a in args)
    shapes = [jax.ShapeDtypeStruct(*shape) for shape in shapes]
    results = pl.pallas_call(
        kernel,
        out_shape=shapes,
        in_specs=specs,
        out_specs=[vmem() for _ in shapes],
        scratch_shapes=list(scratch),
        compiler_params=pltpu.CompilerParams(vmem_limit_bytes=limit),
        cost_estimate=pl.CostEstimate(flops=2**24, bytes_accessed=size, transcendentals=0),
        name=name,
    )(*args)
    return results if len(shapes) > 1 else results[0]


def codes_of(block_row):
    owner, slot = block_row // ROWS, block_row % ROWS
    piece = owner // NY % NX * NYL + owner % NYL
    member = owner // (NX * NY) * NYH + owner % NY // NYL
    return (piece * PIECE + member * BS) * 2**14 + (piece * PIECE + NP * BS + member) * 4 + slot


def local(density, columns, fill_columns):
    f32 = jnp.float32
    tile, copies = call(
        pack_kernel, "pack", [((TILE, LANES), f32), ((NP, TILE, LANES), f32)], [smem(), smem(), vmem()],
        (columns.reshape(1, ROWS), fill_columns.reshape(ROWS, KF), density.reshape(ROWS, BS, BS)),
        limit=60 * 2**20,
    )
    plane = lax.all_to_all(copies, FIRST, 0, 0)
    pair = lax.all_gather(tile, "c")
    plane, pair = lax.optimization_barrier((plane, pair))
    pieces = call(spread_kernel, "spread", [((NS, PIECE, LANES), f32)], [vmem()], (plane,))
    slab = lax.all_to_all(pieces, SECOND, 0, 0).reshape(NS * PIECE, LANES)

    near = [pair] + [
        lax.ppermute(pair, "zl", [(n, (n + step) % NL) for n in range(NL)]) for step in range(1, NL)
    ]
    rows = jnp.stack(near).reshape(NCG, TILE, LANES)
    numbers = rows[:, BS : BS + 5, ::BS].astype(jnp.int32)
    place_here, core = lax.axis_index("zl"), lax.axis_index("c")
    steps = jnp.arange(NCG, dtype=jnp.int32)
    groups = ((place_here - steps // NC) % NL * NC + steps % NC) * CB
    first = codes_of(numbers[:, 0, :].T + groups[None, :]).reshape(-1)
    second = codes_of(numbers[:, 1:, :].transpose(1, 0, 2) + groups[None, :, None])
    second = second.reshape(ROWS, NL, NC, KF)
    places = jnp.arange(NL, dtype=jnp.int32)
    turn = ((place_here - places[:, None]) % NL == places[None, :])[None, :, :, None, None]
    second = jnp.sum(jnp.where(turn, second[:, None], 0), axis=2)
    second = jnp.where(core == 0, second, second[:, :, ::-1]).reshape(-1)
    left = rows[:, :BS].reshape(NCG, BS, ROWS, BS).transpose(2, 1, 0, 3).reshape(ROWS, BS, NCG * BS)

    shape = (ROWS * BS, LANES)
    squared, own = call(
        square_kernel, "square", [((NL,) + shape, f32), (shape, f32)], [smem(), vmem(), vmem(), vmem()],
        (first, tile, left, slab),
        [pltpu.VMEM((ROWS * NCG * BS, 2 * LANES), jnp.bfloat16)],
    )
    upper, lower = (
        functools.partial(
            call, functools.partial(right_kernel, start), "right", [((ROWS // 2 * GROUP, 2 * LANES), jnp.bfloat16)],
            [smem(), vmem(), vmem()],
        )
        for start in (0, ROWS // 2)
    )
    mine, upper = lax.optimization_barrier((lax.all_to_all(squared, "zl", 0, 0), upper((second, tile, slab))))
    other = lax.ppermute(mine, "c", [(0, 1), (1, 0)])
    lower = lower((second, tile, slab))
    purified = call(cube_kernel, "cube", [(shape, f32)], [vmem()] * 5, (mine, other, own, upper, lower))
    return purified.reshape(ROWS, 1, BS, LANES)


def solution(mesh):
    fine = Mesh(mesh.devices.reshape(SIZES), AXES)
    grid, depth = ("zh", "x", "yh", "yl"), ("zl", "c")
    in_specs = (P(grid, depth, None, None), P(grid, depth, None), P(grid, depth, None))
    out_specs = P(grid, depth, None, None)
    return jax.shard_map(local, mesh=fine, in_specs=in_specs, out_specs=out_specs, check_vma=False)
```

```python
import functools

import jax
import jax.numpy as jnp
from jax import lax
from jax.experimental import pallas as pl
from jax.experimental.pallas import tpu as pltpu
from jax.sharding import PartitionSpec as P

BS = 32
ROWS = 4
KF = 4
CB = 48
NCG = 8
LANES = 128
TILE = 40
NZ, NX, NYH, NYL, NL, NC = 3, 4, 4, 2, 4, 2
NY = NYH * NYL
FZ, FX, FY, FL = 1, 2, 2, 2


def turned(count, first):
    return [(n + first) % count for n in range(count)]


def device(zh, x, yh, yl):
    return ((zh * NX + x) * NYH + yh) * NYL + yl


FIRST = [
    [device(zh, x, yh, yl) for zh in turned(NZ, FZ) for yh in turned(NYH, FY)]
    for x in range(NX) for yl in range(NYL)
]
SECOND = [
    [device(zh, x, yh, yl) for x in turned(NX, FX) for yl in range(NYL)]
    for zh in range(NZ) for yh in range(NYH)
]
LINES = [[zl * NC + c for zl in turned(NL, FL)] for c in range(NC)]
PAIRS = [[zl * NC + c for c in range(NC)] for zl in range(NL)]
NP, NS = NZ * NYH, NX * NYL
PIECE = NP * BS + 16
GROUP = NCG * KF * BS


def place(slab, codes, wanted):
    lane_slot = lax.broadcasted_iota(jnp.int32, (8, LANES), 1) // BS
    blocks, columns = [], []
    for code in codes:
        keep = lane_slot == (code & 3)
        block = slab[pl.ds(pl.multiple_of(code >> 14, 8), BS), :].reshape(BS // 8, 8, LANES)
        column = jnp.broadcast_to(slab[pl.ds((code >> 2) & 4095, 1), :], (8, LANES))
        blocks.append(jnp.where(keep, block, 0.0))
        columns.append(jnp.where(keep, column, 0.0)[None])
    every = jnp.concatenate(blocks + columns).reshape(-1, LANES)
    every = every + pltpu.roll(every, 64, 1)
    every = every + pltpu.roll(every, 32, 1)
    count = len(codes)
    blocks = every[: count * BS].reshape(count, BS // 8, 8, LANES)
    columns = every[count * BS :].reshape(count, 8, LANES)
    lands = columns == jnp.stack(wanted)
    return jnp.where(lands[:, None], blocks, 0.0).reshape(count * BS, LANES)


def wanted_of(tile, row):
    return jnp.broadcast_to(tile[BS + 1 + row : BS + 2 + row, :], (8, LANES))


def halves(values, axis):
    high = values.astype(jnp.bfloat16)
    low = (values - high.astype(jnp.float32)).astype(jnp.bfloat16)
    return jnp.concatenate([high, low], axis=axis)


def product(total):
    return (total[:BS, :LANES] + total[:BS, LANES:]) + (total[BS:, :LANES] + total[BS:, LANES:])


def pack_kernel(columns, fill, density, out, copies):
    lane_slot = lax.broadcasted_iota(jnp.int32, (8, LANES), 1) // BS
    line = lax.broadcasted_iota(jnp.int32, (8, LANES), 0)
    numbers = jnp.zeros((8, LANES), jnp.int32)
    for slot in range(ROWS):
        numbers = jnp.where((line == 0) & (lane_slot == slot), columns[0, slot], numbers)
    for row in range(ROWS):
        for slot in range(KF):
            numbers = jnp.where((line == row + 1) & (lane_slot == slot), fill[row, slot], numbers)
    numbers = numbers.astype(jnp.float32)
    data = jnp.concatenate([density[row] for row in range(ROWS)], axis=1)
    out[:BS, :] = data
    out[BS:, :] = numbers
    for n in range(NP):
        copies[n, :BS, :] = data
        copies[n, BS:, :] = numbers


def spread_kernel(plane, out):
    for member in range(NP):
        block = plane[member, :BS, :]
        column = plane[member, BS : BS + 1, :]
        for n in range(NS):
            out[n, member * BS : (member + 1) * BS, :] = block
            out[n, NP * BS + member : NP * BS + member + 1, :] = column
    for n in range(NS):
        out[n, NP * BS + NP :, :] = jnp.zeros((PIECE - NP * BS - NP, LANES), jnp.float32)


def square_kernel(codes, tile, left, slab, out, own, right):
    for row in range(0, ROWS, 2):
        wanted = [wanted_of(tile, row)] * NCG + [wanted_of(tile, row + 1)] * NCG
        blocks = place(slab, [codes[row * NCG + t] for t in range(2 * NCG)], wanted)
        right[row * NCG * BS : (row + 2) * NCG * BS, :] = halves(blocks, 1)
    for row in range(ROWS):
        values = right[row * NCG * BS : (row + 1) * NCG * BS, :]
        result = product(jnp.dot(halves(left[row], 0), values, preferred_element_type=jnp.float32))
        rows = slice(row * BS, (row + 1) * BS)
        own[rows, :] = result
        for n in range(NL):
            out[n, rows, :] = result


def right_kernel(start, codes, tile, slab, out):
    batch = 16
    for row in range(ROWS // 2):
        wanted = [wanted_of(tile, start + row)] * batch
        for t in range(row * NCG * KF, (row + 1) * NCG * KF, batch):
            blocks = place(slab, [codes[start * NCG * KF + t + n] for n in range(batch)], wanted)
            out[t * BS : (t + batch) * BS, :] = halves(blocks, 1)


def cube_kernel(mine, other, own, upper, lower, out):
    for row in range(ROWS):
        right = upper if row < ROWS // 2 else lower
        rows = slice(row * BS, (row + 1) * BS)
        total = jnp.zeros((2 * BS, 2 * LANES), jnp.float32)
        for near in range(NL):
            values = jnp.concatenate([mine[near, rows, :], other[near, rows, :]], axis=1)
            start = row % (ROWS // 2) * GROUP + near * NC * LANES
            total = total + jnp.dot(
                halves(values, 0), right[start : start + NC * LANES, :], preferred_element_type=jnp.float32
            )
        out[rows, :] = 3.0 * own[rows, :] - 2.0 * product(total)


def vmem():
    return pl.BlockSpec(memory_space=pltpu.VMEM)


def smem():
    return pl.BlockSpec(memory_space=pltpu.SMEM)


def call(kernel, name, shapes, specs, args, scratch=(), limit=16 * 2**20):
    size = 4 * sum(a.size for a in args)
    shapes = [jax.ShapeDtypeStruct(*shape) for shape in shapes]
    results = pl.pallas_call(
        kernel,
        out_shape=shapes,
        in_specs=specs,
        out_specs=[vmem() for _ in shapes],
        scratch_shapes=list(scratch),
        compiler_params=pltpu.CompilerParams(vmem_limit_bytes=limit),
        cost_estimate=pl.CostEstimate(flops=2**24, bytes_accessed=size, transcendentals=0),
        name=name,
    )(*args)
    return results if len(shapes) > 1 else results[0]


def codes_of(block_row):
    owner, slot = block_row // ROWS, block_row % ROWS
    piece = (owner // NY - FX) % NX * NYL + owner % NYL
    member = (owner // (NX * NY) - FZ) % NZ * NYH + (owner % NY // NYL - FY) % NYH
    return (piece * PIECE + member * BS) * 2**14 + (piece * PIECE + NP * BS + member) * 4 + slot


def local(density, columns, fill_columns):
    f32 = jnp.float32
    tile, copies = call(
        pack_kernel, "pack", [((TILE, LANES), f32), ((NP, TILE, LANES), f32)], [smem(), smem(), vmem()],
        (columns.reshape(1, ROWS), fill_columns.reshape(ROWS, KF), density.reshape(ROWS, BS, BS)),
        limit=60 * 2**20,
    )
    plane = lax.all_to_all(copies, "grid", 0, 0, axis_index_groups=FIRST)
    pair = lax.all_gather(tile, "depth", axis_index_groups=PAIRS)
    plane, pair = lax.optimization_barrier((plane, pair))
    pieces = call(spread_kernel, "spread", [((NS, PIECE, LANES), f32)], [vmem()], (plane,))
    slab = lax.all_to_all(pieces, "grid", 0, 0, axis_index_groups=SECOND).reshape(NS * PIECE, LANES)

    near = [pair] + [
        lax.ppermute(pair, "depth", [(n, (n + step * NC) % NCG) for n in range(NCG)]) for step in range(1, NL)
    ]
    rows = jnp.stack(near).reshape(NCG, TILE, LANES)
    numbers = rows[:, BS : BS + 5, ::BS].astype(jnp.int32)
    place_here, core = lax.axis_index("depth") // NC, lax.axis_index("depth") % NC
    steps = jnp.arange(NCG, dtype=jnp.int32)
    groups = ((place_here - steps // NC) % NL * NC + steps % NC) * CB
    first = codes_of(numbers[:, 0, :].T + groups[None, :]).reshape(-1)
    second = codes_of(numbers[:, 1:, :].transpose(1, 0, 2) + groups[None, :, None])
    second = second.reshape(ROWS, NL, NC, KF)
    places, lines = jnp.arange(NL, dtype=jnp.int32), jnp.array(turned(NL, FL), dtype=jnp.int32)
    turn = ((place_here - lines[:, None]) % NL == places[None, :])[None, :, :, None, None]
    second = jnp.sum(jnp.where(turn, second[:, None], 0), axis=2)
    second = jnp.where(core == 0, second, second[:, :, ::-1]).reshape(-1)
    left = rows[:, :BS].reshape(NCG, BS, ROWS, BS).transpose(2, 1, 0, 3).reshape(ROWS, BS, NCG * BS)

    shape = (ROWS * BS, LANES)
    squared, own = call(
        square_kernel, "square", [((NL,) + shape, f32), (shape, f32)], [smem(), vmem(), vmem(), vmem()],
        (first, tile, left, slab),
        [pltpu.VMEM((ROWS * NCG * BS, 2 * LANES), jnp.bfloat16)],
    )
    upper, lower = (
        functools.partial(
            call, functools.partial(right_kernel, start), "right", [((ROWS // 2 * GROUP, 2 * LANES), jnp.bfloat16)],
            [smem(), vmem(), vmem()],
        )
        for start in (0, ROWS // 2)
    )
    mine, upper = lax.optimization_barrier((lax.all_to_all(squared, "depth", 0, 0, axis_index_groups=LINES), upper((second, tile, slab))))
    other = lax.ppermute(mine, "depth", [(n, n ^ 1) for n in range(NCG)])
    lower = lower((second, tile, slab))
    purified = call(cube_kernel, "cube", [(shape, f32)], [vmem()] * 5, (mine, other, own, upper, lower))
    return purified.reshape(ROWS, 1, BS, LANES)


def solution(mesh):
    blocks, pattern = P("grid", "depth", None, None), P("grid", "depth", None)
    return jax.shard_map(
        local, mesh=mesh, in_specs=(blocks, pattern, pattern), out_specs=blocks, check_vma=False
    )
```

```python
import functools

import jax
import jax.numpy as jnp
from jax import lax
from jax.experimental import pallas as pl
from jax.experimental.pallas import tpu as pltpu
from jax.sharding import PartitionSpec as P

BS = 32
ROWS = 4
KF = 4
CB = 48
NCG = 8
LANES = 128
TILE = 40
NZ, NX, NYH, NYL, NL, NC = 3, 4, 4, 2, 4, 2
NY = NYH * NYL
FZ, FX, FY, FL = 2, 3, 2, 2


def turned(count, first):
    return [(n + first) % count for n in range(count)]


def device(zh, x, yh, yl):
    return ((zh * NX + x) * NYH + yh) * NYL + yl


FIRST = [
    [device(zh, x, yh, yl) for zh in turned(NZ, FZ) for yh in turned(NYH, FY)]
    for x in range(NX) for yl in range(NYL)
]
SECOND = [
    [device(zh, x, yh, yl) for x in turned(NX, FX) for yl in range(NYL)]
    for zh in range(NZ) for yh in range(NYH)
]
LINES = [[zl * NC + c for zl in turned(NL, FL)] for c in range(NC)]
PAIRS = [[zl * NC + c for c in range(NC)] for zl in range(NL)]
NP, NS = NZ * NYH, NX * NYL
PIECE = NP * BS + 16
GROUP = NCG * KF * BS


def place(slab, codes, wanted):
    lane_slot = lax.broadcasted_iota(jnp.int32, (8, LANES), 1) // BS
    blocks, columns = [], []
    for code in codes:
        keep = lane_slot == (code & 3)
        block = slab[pl.ds(pl.multiple_of(code >> 14, 8), BS), :].reshape(BS // 8, 8, LANES)
        column = jnp.broadcast_to(slab[pl.ds((code >> 2) & 4095, 1), :], (8, LANES))
        blocks.append(jnp.where(keep, block, 0.0))
        columns.append(jnp.where(keep, column, 0.0)[None])
    every = jnp.concatenate(blocks + columns).reshape(-1, LANES)
    every = every + pltpu.roll(every, 64, 1)
    every = every + pltpu.roll(every, 32, 1)
    count = len(codes)
    blocks = every[: count * BS].reshape(count, BS // 8, 8, LANES)
    columns = every[count * BS :].reshape(count, 8, LANES)
    lands = columns == jnp.stack(wanted)
    return jnp.where(lands[:, None], blocks, 0.0).reshape(count * BS, LANES)


def wanted_of(tile, row):
    return jnp.broadcast_to(tile[BS + 1 + row : BS + 2 + row, :], (8, LANES))


def halves(values, axis):
    high = values.astype(jnp.bfloat16)
    low = (values - high.astype(jnp.float32)).astype(jnp.bfloat16)
    return jnp.concatenate([high, low], axis=axis)


def product(total):
    return (total[:BS, :LANES] + total[:BS, LANES:]) + (total[BS:, :LANES] + total[BS:, LANES:])


def pack_kernel(columns, fill, density, out, copies):
    lane_slot = lax.broadcasted_iota(jnp.int32, (8, LANES), 1) // BS
    line = lax.broadcasted_iota(jnp.int32, (8, LANES), 0)
    numbers = jnp.zeros((8, LANES), jnp.int32)
    for slot in range(ROWS):
        numbers = jnp.where((line == 0) & (lane_slot == slot), columns[0, slot], numbers)
    for row in range(ROWS):
        for slot in range(KF):
            numbers = jnp.where((line == row + 1) & (lane_slot == slot), fill[row, slot], numbers)
    numbers = numbers.astype(jnp.float32)
    data = jnp.concatenate([density[row] for row in range(ROWS)], axis=1)
    out[:BS, :] = data
    out[BS:, :] = numbers
    for n in range(NP):
        copies[n, :BS, :] = data
        copies[n, BS:, :] = numbers


def spread_kernel(plane, out):
    for member in range(NP):
        block = plane[member, :BS, :]
        column = plane[member, BS : BS + 1, :]
        for n in range(NS):
            out[n, member * BS : (member + 1) * BS, :] = block
            out[n, NP * BS + member : NP * BS + member + 1, :] = column
    for n in range(NS):
        out[n, NP * BS + NP :, :] = jnp.zeros((PIECE - NP * BS - NP, LANES), jnp.float32)


def square_kernel(codes, tile, left, slab, out, own, right):
    for row in range(0, ROWS, 2):
        wanted = [wanted_of(tile, row)] * NCG + [wanted_of(tile, row + 1)] * NCG
        blocks = place(slab, [codes[row * NCG + t] for t in range(2 * NCG)], wanted)
        right[row * NCG * BS : (row + 2) * NCG * BS, :] = halves(blocks, 1)
    for row in range(ROWS):
        values = right[row * NCG * BS : (row + 1) * NCG * BS, :]
        result = product(jnp.dot(halves(left[row], 0), values, preferred_element_type=jnp.float32))
        rows = slice(row * BS, (row + 1) * BS)
        own[rows, :] = result
        for n in range(NL):
            out[n, rows, :] = result


def right_kernel(start, codes, tile, slab, out):
    batch = 16
    for row in range(ROWS // 2):
        wanted = [wanted_of(tile, start + row)] * batch
        for t in range(row * NCG * KF, (row + 1) * NCG * KF, batch):
            blocks = place(slab, [codes[start * NCG * KF + t + n] for n in range(batch)], wanted)
            out[t * BS : (t + batch) * BS, :] = halves(blocks, 1)


def cube_kernel(mine, other, own, upper, lower, out):
    for row in range(ROWS):
        right = upper if row < ROWS // 2 else lower
        rows = slice(row * BS, (row + 1) * BS)
        total = jnp.zeros((2 * BS, 2 * LANES), jnp.float32)
        for near in range(NL):
            values = jnp.concatenate([mine[near, rows, :], other[near, rows, :]], axis=1)
            start = row % (ROWS // 2) * GROUP + near * NC * LANES
            total = total + jnp.dot(
                halves(values, 0), right[start : start + NC * LANES, :], preferred_element_type=jnp.float32
            )
        out[rows, :] = 3.0 * own[rows, :] - 2.0 * product(total)


def vmem():
    return pl.BlockSpec(memory_space=pltpu.VMEM)


def smem():
    return pl.BlockSpec(memory_space=pltpu.SMEM)


def call(kernel, name, shapes, specs, args, scratch=(), limit=16 * 2**20):
    size = 4 * sum(a.size for a in args)
    shapes = [jax.ShapeDtypeStruct(*shape) for shape in shapes]
    results = pl.pallas_call(
        kernel,
        out_shape=shapes,
        in_specs=specs,
        out_specs=[vmem() for _ in shapes],
        scratch_shapes=list(scratch),
        compiler_params=pltpu.CompilerParams(vmem_limit_bytes=limit),
        cost_estimate=pl.CostEstimate(flops=2**24, bytes_accessed=size, transcendentals=0),
        name=name,
    )(*args)
    return results if len(shapes) > 1 else results[0]


def codes_of(block_row):
    owner, slot = block_row // ROWS, block_row % ROWS
    piece = (owner // NY - FX) % NX * NYL + owner % NYL
    member = (owner // (NX * NY) - FZ) % NZ * NYH + (owner % NY // NYL - FY) % NYH
    return (piece * PIECE + member * BS) * 2**14 + (piece * PIECE + NP * BS + member) * 4 + slot


def local(density, columns, fill_columns):
    f32 = jnp.float32
    tile, copies = call(
        pack_kernel, "pack", [((TILE, LANES), f32), ((NP, TILE, LANES), f32)], [smem(), smem(), vmem()],
        (columns.reshape(1, ROWS), fill_columns.reshape(ROWS, KF), density.reshape(ROWS, BS, BS)),
        limit=60 * 2**20,
    )
    plane = lax.all_to_all(copies, "grid", 0, 0, axis_index_groups=FIRST)
    pair = lax.all_gather(tile, "depth", axis_index_groups=PAIRS)
    plane, pair = lax.optimization_barrier((plane, pair))
    pieces = call(spread_kernel, "spread", [((NS, PIECE, LANES), f32)], [vmem()], (plane,))
    slab = lax.all_to_all(pieces, "grid", 0, 0, axis_index_groups=SECOND).reshape(NS * PIECE, LANES)

    near = [pair] + [
        lax.ppermute(pair, "depth", [(n, (n + step * NC) % NCG) for n in range(NCG)]) for step in range(1, NL)
    ]
    rows = jnp.stack(near).reshape(NCG, TILE, LANES)
    numbers = rows[:, BS : BS + 5, ::BS].astype(jnp.int32)
    place_here, core = lax.axis_index("depth") // NC, lax.axis_index("depth") % NC
    steps = jnp.arange(NCG, dtype=jnp.int32)
    groups = ((place_here - steps // NC) % NL * NC + steps % NC) * CB
    first = codes_of(numbers[:, 0, :].T + groups[None, :]).reshape(-1)
    second = codes_of(numbers[:, 1:, :].transpose(1, 0, 2) + groups[None, :, None])
    second = second.reshape(ROWS, NL, NC, KF)
    places, lines = jnp.arange(NL, dtype=jnp.int32), jnp.array(turned(NL, FL), dtype=jnp.int32)
    turn = ((place_here - lines[:, None]) % NL == places[None, :])[None, :, :, None, None]
    second = jnp.sum(jnp.where(turn, second[:, None], 0), axis=2)
    second = jnp.where(core == 0, second, second[:, :, ::-1]).reshape(-1)
    left = rows[:, :BS].reshape(NCG, BS, ROWS, BS).transpose(2, 1, 0, 3).reshape(ROWS, BS, NCG * BS)

    shape = (ROWS * BS, LANES)
    squared, own = call(
        square_kernel, "square", [((NL,) + shape, f32), (shape, f32)], [smem(), vmem(), vmem(), vmem()],
        (first, tile, left, slab),
        [pltpu.VMEM((ROWS * NCG * BS, 2 * LANES), jnp.bfloat16)],
    )
    upper, lower = (
        functools.partial(
            call, functools.partial(right_kernel, start), "right", [((ROWS // 2 * GROUP, 2 * LANES), jnp.bfloat16)],
            [smem(), vmem(), vmem()],
        )
        for start in (0, ROWS // 2)
    )
    mine, upper = lax.optimization_barrier((lax.all_to_all(squared, "depth", 0, 0, axis_index_groups=LINES), upper((second, tile, slab))))
    other = lax.ppermute(mine, "depth", [(n, n ^ 1) for n in range(NCG)])
    lower = lower((second, tile, slab))
    purified = call(cube_kernel, "cube", [(shape, f32)], [vmem()] * 5, (mine, other, own, upper, lower))
    return purified.reshape(ROWS, 1, BS, LANES)


def solution(mesh):
    blocks, pattern = P("grid", "depth", None, None), P("grid", "depth", None)
    return jax.shard_map(
        local, mesh=mesh, in_specs=(blocks, pattern, pattern), out_specs=blocks, check_vma=False
    )
```

```python
import functools

import jax
import jax.numpy as jnp
from jax import lax
from jax.experimental import pallas as pl
from jax.experimental.pallas import tpu as pltpu
from jax.sharding import PartitionSpec as P

BS = 32
ROWS = 4
KF = 4
CB = 48
NCG = 8
LANES = 128
TILE = 40
NZ, NX, NYH, NYL, NL, NC = 3, 4, 4, 2, 4, 2
NY = NYH * NYL
FZ, FX, FY, FL = 2, 3, 2, 2


def turned(count, first):
    return [(n + first) % count for n in range(count)]


def device(zh, x, yh, yl):
    return ((zh * NX + x) * NYH + yh) * NYL + yl


FIRST = [
    [device(zh, x, yh, yl) for zh in turned(NZ, FZ) for yh in turned(NYH, FY)]
    for x in range(NX) for yl in range(NYL)
]
SECOND = [
    [device(zh, x, yh, yl) for x in turned(NX, FX) for yl in range(NYL)]
    for zh in range(NZ) for yh in range(NYH)
]
LINES = [[zl * NC + c for zl in turned(NL, FL)] for c in range(NC)]
PAIRS = [[zl * NC + c for c in range(NC)] for zl in range(NL)]
NP, NS = NZ * NYH, NX * NYL
PIECE = NP * BS + 16
GROUP = NCG * KF * BS


def place(slab, codes, wanted):
    lane_slot = lax.broadcasted_iota(jnp.int32, (8, LANES), 1) // BS
    blocks, columns = [], []
    for code in codes:
        keep = lane_slot == (code & 3)
        block = slab[pl.ds(pl.multiple_of(code >> 14, 8), BS), :].reshape(BS // 8, 8, LANES)
        column = jnp.broadcast_to(slab[pl.ds((code >> 2) & 4095, 1), :], (8, LANES))
        blocks.append(jnp.where(keep, block, 0.0))
        columns.append(jnp.where(keep, column, 0.0)[None])
    every = jnp.concatenate(blocks + columns).reshape(-1, LANES)
    every = every + pltpu.roll(every, 64, 1)
    every = every + pltpu.roll(every, 32, 1)
    count = len(codes)
    blocks = every[: count * BS].reshape(count, BS // 8, 8, LANES)
    columns = every[count * BS :].reshape(count, 8, LANES)
    lands = columns == jnp.stack(wanted)
    return jnp.where(lands[:, None], blocks, 0.0).reshape(count * BS, LANES)


def wanted_of(tile, row):
    return jnp.broadcast_to(tile[BS + 1 + row : BS + 2 + row, :], (8, LANES))


def halves(values, axis):
    high = values.astype(jnp.bfloat16)
    low = (values - high.astype(jnp.float32)).astype(jnp.bfloat16)
    return jnp.concatenate([high, low], axis=axis)


def product(total):
    return (total[:BS, :LANES] + total[:BS, LANES:]) + (total[BS:, :LANES] + total[BS:, LANES:])


def pack_kernel(columns, fill, density, out, copies):
    lane_slot = lax.broadcasted_iota(jnp.int32, (8, LANES), 1) // BS
    line = lax.broadcasted_iota(jnp.int32, (8, LANES), 0)
    numbers = jnp.zeros((8, LANES), jnp.int32)
    for slot in range(ROWS):
        numbers = jnp.where((line == 0) & (lane_slot == slot), columns[0, slot], numbers)
    for row in range(ROWS):
        for slot in range(KF):
            numbers = jnp.where((line == row + 1) & (lane_slot == slot), fill[row, slot], numbers)
    numbers = numbers.astype(jnp.float32)
    data = jnp.concatenate([density[row] for row in range(ROWS)], axis=1)
    out[:BS, :] = data
    out[BS:, :] = numbers
    for n in range(NP):
        copies[n, :BS, 0, :] = data
        copies[n, BS:, 0, :] = numbers[:1]


def spread_kernel(plane, out):
    for member in range(NP):
        block = plane[member, :BS, 0, :]
        column = plane[member, BS:, 0, :]
        for n in range(NS):
            out[n, member * BS : (member + 1) * BS, :] = block
            out[n, NP * BS + member : NP * BS + member + 1, :] = column
    for n in range(NS):
        out[n, NP * BS + NP :, :] = jnp.zeros((PIECE - NP * BS - NP, LANES), jnp.float32)


def square_kernel(codes, tile, left, slab, out, own, right):
    for row in range(0, ROWS, 2):
        wanted = [wanted_of(tile, row)] * NCG + [wanted_of(tile, row + 1)] * NCG
        blocks = place(slab, [codes[row * NCG + t] for t in range(2 * NCG)], wanted)
        right[row * NCG * BS : (row + 2) * NCG * BS, :] = halves(blocks, 1)
    for row in range(ROWS):
        values = right[row * NCG * BS : (row + 1) * NCG * BS, :]
        result = product(jnp.dot(halves(left[row], 0), values, preferred_element_type=jnp.float32))
        rows = slice(row * BS, (row + 1) * BS)
        own[rows, :] = result
        for n in range(NL):
            out[n, rows, :] = result


def right_kernel(start, codes, tile, slab, out):
    batch = 16
    for row in range(ROWS // 2):
        wanted = [wanted_of(tile, start + row)] * batch
        for t in range(row * NCG * KF, (row + 1) * NCG * KF, batch):
            blocks = place(slab, [codes[start * NCG * KF + t + n] for n in range(batch)], wanted)
            out[t * BS : (t + batch) * BS, :] = halves(blocks, 1)


def cube_kernel(mine, other, own, upper, lower, out):
    for row in range(ROWS):
        right = upper if row < ROWS // 2 else lower
        rows = slice(row * BS, (row + 1) * BS)
        total = jnp.zeros((2 * BS, 2 * LANES), jnp.float32)
        for near in range(NL):
            values = jnp.concatenate([mine[near, rows, :], other[near, rows, :]], axis=1)
            start = row % (ROWS // 2) * GROUP + near * NC * LANES
            total = total + jnp.dot(
                halves(values, 0), right[start : start + NC * LANES, :], preferred_element_type=jnp.float32
            )
        out[rows, :] = 3.0 * own[rows, :] - 2.0 * product(total)


def vmem():
    return pl.BlockSpec(memory_space=pltpu.VMEM)


def smem():
    return pl.BlockSpec(memory_space=pltpu.SMEM)


def call(kernel, name, shapes, specs, args, scratch=(), limit=16 * 2**20):
    size = 4 * sum(a.size for a in args)
    shapes = [jax.ShapeDtypeStruct(*shape) for shape in shapes]
    results = pl.pallas_call(
        kernel,
        out_shape=shapes,
        in_specs=specs,
        out_specs=[vmem() for _ in shapes],
        scratch_shapes=list(scratch),
        compiler_params=pltpu.CompilerParams(vmem_limit_bytes=limit),
        cost_estimate=pl.CostEstimate(flops=2**24, bytes_accessed=size, transcendentals=0),
        name=name,
    )(*args)
    return results if len(shapes) > 1 else results[0]


def codes_of(block_row):
    owner, slot = block_row // ROWS, block_row % ROWS
    piece = (owner // NY - FX) % NX * NYL + owner % NYL
    member = (owner // (NX * NY) - FZ) % NZ * NYH + (owner % NY // NYL - FY) % NYH
    return (piece * PIECE + member * BS) * 2**14 + (piece * PIECE + NP * BS + member) * 4 + slot


def local(density, columns, fill_columns):
    f32 = jnp.float32
    tile, copies = call(
        pack_kernel, "pack", [((TILE, LANES), f32), ((NP, BS + 1, 1, LANES), f32)], [smem(), smem(), vmem()],
        (columns.reshape(1, ROWS), fill_columns.reshape(ROWS, KF), density.reshape(ROWS, BS, BS)),
        limit=60 * 2**20,
    )
    plane = lax.all_to_all(copies, "grid", 0, 0, axis_index_groups=FIRST)
    pair = lax.all_gather(tile, "depth", axis_index_groups=PAIRS)
    plane, pair = lax.optimization_barrier((plane, pair))
    pieces = call(spread_kernel, "spread", [((NS, PIECE, LANES), f32)], [vmem()], (plane,))
    slab = lax.all_to_all(pieces, "grid", 0, 0, axis_index_groups=SECOND).reshape(NS * PIECE, LANES)

    near = [pair] + [
        lax.ppermute(pair, "depth", [(n, (n + step * NC) % NCG) for n in range(NCG)]) for step in range(1, NL)
    ]
    rows = jnp.stack(near).reshape(NCG, TILE, LANES)
    numbers = rows[:, BS : BS + 5, ::BS].astype(jnp.int32)
    place_here, core = lax.axis_index("depth") // NC, lax.axis_index("depth") % NC
    steps = jnp.arange(NCG, dtype=jnp.int32)
    groups = ((place_here - steps // NC) % NL * NC + steps % NC) * CB
    first = codes_of(numbers[:, 0, :].T + groups[None, :]).reshape(-1)
    second = codes_of(numbers[:, 1:, :].transpose(1, 0, 2) + groups[None, :, None])
    second = second.reshape(ROWS, NL, NC, KF)
    places, lines = jnp.arange(NL, dtype=jnp.int32), jnp.array(turned(NL, FL), dtype=jnp.int32)
    turn = ((place_here - lines[:, None]) % NL == places[None, :])[None, :, :, None, None]
    second = jnp.sum(jnp.where(turn, second[:, None], 0), axis=2)
    second = jnp.where(core == 0, second, second[:, :, ::-1]).reshape(-1)
    left = rows[:, :BS].reshape(NCG, BS, ROWS, BS).transpose(2, 1, 0, 3).reshape(ROWS, BS, NCG * BS)

    shape = (ROWS * BS, LANES)
    squared, own = call(
        square_kernel, "square", [((NL,) + shape, f32), (shape, f32)], [smem(), vmem(), vmem(), vmem()],
        (first, tile, left, slab),
        [pltpu.VMEM((ROWS * NCG * BS, 2 * LANES), jnp.bfloat16)],
    )
    upper, lower = (
        functools.partial(
            call, functools.partial(right_kernel, start), "right", [((ROWS // 2 * GROUP, 2 * LANES), jnp.bfloat16)],
            [smem(), vmem(), vmem()],
        )
        for start in (0, ROWS // 2)
    )
    mine, upper = lax.optimization_barrier((lax.all_to_all(squared, "depth", 0, 0, axis_index_groups=LINES), upper((second, tile, slab))))
    other = lax.ppermute(mine, "depth", [(n, n ^ 1) for n in range(NCG)])
    lower = lower((second, tile, slab))
    purified = call(cube_kernel, "cube", [(shape, f32)], [vmem()] * 5, (mine, other, own, upper, lower))
    return purified.reshape(ROWS, 1, BS, LANES)


def solution(mesh):
    blocks, pattern = P("grid", "depth", None, None), P("grid", "depth", None)
    return jax.shard_map(
        local, mesh=mesh, in_specs=(blocks, pattern, pattern), out_specs=blocks, check_vma=False
    )
```

```python
import functools

import jax
import jax.numpy as jnp
from jax import lax
from jax.experimental import pallas as pl
from jax.experimental.pallas import tpu as pltpu
from jax.sharding import PartitionSpec as P

BS = 32
ROWS = 4
KF = 4
CB = 48
NCG = 8
LANES = 128
TILE = 40
NZ, NX, NYH, NYL, NL, NC = 3, 4, 4, 2, 4, 2
NY = NYH * NYL
FZ, FX, FY, FL = 2, 3, 3, 2


def turned(count, first):
    return [(n + first) % count for n in range(count)]


def device(zh, x, yh, yl):
    return ((zh * NX + x) * NYH + yh) * NYL + yl


FIRST = [
    [device(zh, x, yh, yl) for zh in turned(NZ, FZ) for yh in turned(NYH, FY)]
    for x in range(NX) for yl in range(NYL)
]
SECOND = [
    [device(zh, x, yh, yl) for x in turned(NX, FX) for yl in range(NYL)]
    for zh in range(NZ) for yh in range(NYH)
]
LINES = [[zl * NC + c for zl in turned(NL, FL)] for c in range(NC)]
PAIRS = [[zl * NC + c for c in range(NC)] for zl in range(NL)]
NP, NS = NZ * NYH, NX * NYL
PIECE = NP * BS + 16
GROUP = NCG * KF * BS


def place(slab, codes, wanted):
    lane_slot = lax.broadcasted_iota(jnp.int32, (8, LANES), 1) // BS
    blocks, columns = [], []
    for code in codes:
        keep = lane_slot == (code & 3)
        block = slab[pl.ds(pl.multiple_of(code >> 14, 8), BS), :].reshape(BS // 8, 8, LANES)
        column = jnp.broadcast_to(slab[pl.ds((code >> 2) & 4095, 1), :], (8, LANES))
        blocks.append(jnp.where(keep, block, 0.0))
        columns.append(jnp.where(keep, column, 0.0)[None])
    every = jnp.concatenate(blocks + columns).reshape(-1, LANES)
    every = every + pltpu.roll(every, 64, 1)
    every = every + pltpu.roll(every, 32, 1)
    count = len(codes)
    blocks = every[: count * BS].reshape(count, BS // 8, 8, LANES)
    columns = every[count * BS :].reshape(count, 8, LANES)
    lands = columns == jnp.stack(wanted)
    return jnp.where(lands[:, None], blocks, 0.0).reshape(count * BS, LANES)


def wanted_of(tile, row):
    return jnp.broadcast_to(tile[BS + 1 + row : BS + 2 + row, :], (8, LANES))


def halves(values, axis):
    high = values.astype(jnp.bfloat16)
    low = (values - high.astype(jnp.float32)).astype(jnp.bfloat16)
    return jnp.concatenate([high, low], axis=axis)


def product(total):
    return (total[:BS, :LANES] + total[:BS, LANES:]) + (total[BS:, :LANES] + total[BS:, LANES:])


def pack_kernel(columns, fill, density, out, copies):
    lane_slot = lax.broadcasted_iota(jnp.int32, (8, LANES), 1) // BS
    line = lax.broadcasted_iota(jnp.int32, (8, LANES), 0)
    numbers = jnp.zeros((8, LANES), jnp.int32)
    for slot in range(ROWS):
        numbers = jnp.where((line == 0) & (lane_slot == slot), columns[0, slot], numbers)
    for row in range(ROWS):
        for slot in range(KF):
            numbers = jnp.where((line == row + 1) & (lane_slot == slot), fill[row, slot], numbers)
    numbers = numbers.astype(jnp.float32)
    data = jnp.concatenate([density[row] for row in range(ROWS)], axis=1)
    out[:BS, :] = data
    out[BS:, :] = numbers
    for n in range(NP):
        copies[n, :BS, 0, :] = data
        copies[n, BS:, 0, :] = numbers[:1]


def spread_kernel(plane, out):
    for member in range(NP):
        block = plane[member, :BS, 0, :]
        column = plane[member, BS:, 0, :]
        for n in range(NS):
            out[n, member * BS : (member + 1) * BS, :] = block
            out[n, NP * BS + member : NP * BS + member + 1, :] = column
    for n in range(NS):
        out[n, NP * BS + NP :, :] = jnp.zeros((PIECE - NP * BS - NP, LANES), jnp.float32)


def square_kernel(codes, tile, left, slab, out, own, right):
    for row in range(0, ROWS, 2):
        wanted = [wanted_of(tile, row)] * NCG + [wanted_of(tile, row + 1)] * NCG
        blocks = place(slab, [codes[row * NCG + t] for t in range(2 * NCG)], wanted)
        right[row * NCG * BS : (row + 2) * NCG * BS, :] = halves(blocks, 1)
    for row in range(ROWS):
        values = right[row * NCG * BS : (row + 1) * NCG * BS, :]
        result = product(jnp.dot(halves(left[row], 0), values, preferred_element_type=jnp.float32))
        rows = slice(row * BS, (row + 1) * BS)
        own[rows, :] = result
        for n in range(NL):
            out[n, rows, :] = result


def right_kernel(start, codes, tile, slab, out):
    batch = 16
    for row in range(ROWS // 2):
        wanted = [wanted_of(tile, start + row)] * batch
        for t in range(row * NCG * KF, (row + 1) * NCG * KF, batch):
            blocks = place(slab, [codes[start * NCG * KF + t + n] for n in range(batch)], wanted)
            out[t * BS : (t + batch) * BS, :] = halves(blocks, 1)


def cube_kernel(mine, other, own, upper, lower, out):
    for row in range(ROWS):
        right = upper if row < ROWS // 2 else lower
        rows = slice(row * BS, (row + 1) * BS)
        total = jnp.zeros((2 * BS, 2 * LANES), jnp.float32)
        for near in range(NL):
            values = jnp.concatenate([mine[near, rows, :], other[near, rows, :]], axis=1)
            start = row % (ROWS // 2) * GROUP + near * NC * LANES
            total = total + jnp.dot(
                halves(values, 0), right[start : start + NC * LANES, :], preferred_element_type=jnp.float32
            )
        out[rows, :] = 3.0 * own[rows, :] - 2.0 * product(total)


def vmem():
    return pl.BlockSpec(memory_space=pltpu.VMEM)


def smem():
    return pl.BlockSpec(memory_space=pltpu.SMEM)


def call(kernel, name, shapes, specs, args, scratch=(), limit=16 * 2**20):
    size = 4 * sum(a.size for a in args)
    shapes = [jax.ShapeDtypeStruct(*shape) for shape in shapes]
    results = pl.pallas_call(
        kernel,
        out_shape=shapes,
        in_specs=specs,
        out_specs=[vmem() for _ in shapes],
        scratch_shapes=list(scratch),
        compiler_params=pltpu.CompilerParams(vmem_limit_bytes=limit),
        cost_estimate=pl.CostEstimate(flops=2**24, bytes_accessed=size, transcendentals=0),
        name=name,
    )(*args)
    return results if len(shapes) > 1 else results[0]


def codes_of(block_row):
    owner, slot = block_row // ROWS, block_row % ROWS
    piece = (owner // NY - FX) % NX * NYL + owner % NYL
    member = (owner // (NX * NY) - FZ) % NZ * NYH + (owner % NY // NYL - FY) % NYH
    return (piece * PIECE + member * BS) * 2**14 + (piece * PIECE + NP * BS + member) * 4 + slot


def local(density, columns, fill_columns):
    f32 = jnp.float32
    tile, copies = call(
        pack_kernel, "pack", [((TILE, LANES), f32), ((NP, BS + 1, 1, LANES), f32)], [smem(), smem(), vmem()],
        (columns.reshape(1, ROWS), fill_columns.reshape(ROWS, KF), density.reshape(ROWS, BS, BS)),
        limit=60 * 2**20,
    )
    plane = lax.all_to_all(copies, "grid", 0, 0, axis_index_groups=FIRST)
    pair = lax.all_gather(tile, "depth", axis_index_groups=PAIRS)
    plane, pair = lax.optimization_barrier((plane, pair))
    pieces = call(spread_kernel, "spread", [((NS, PIECE, LANES), f32)], [vmem()], (plane,))
    slab = lax.all_to_all(pieces, "grid", 0, 0, axis_index_groups=SECOND).reshape(NS * PIECE, LANES)

    near = [pair] + [
        lax.ppermute(pair, "depth", [(n, (n + step * NC) % NCG) for n in range(NCG)]) for step in range(1, NL)
    ]
    rows = jnp.stack(near).reshape(NCG, TILE, LANES)
    numbers = rows[:, BS : BS + 5, ::BS].astype(jnp.int32)
    place_here, core = lax.axis_index("depth") // NC, lax.axis_index("depth") % NC
    steps = jnp.arange(NCG, dtype=jnp.int32)
    groups = ((place_here - steps // NC) % NL * NC + steps % NC) * CB
    first = codes_of(numbers[:, 0, :].T + groups[None, :]).reshape(-1)
    second = codes_of(numbers[:, 1:, :].transpose(1, 0, 2) + groups[None, :, None])
    second = second.reshape(ROWS, NL, NC, KF)
    places, lines = jnp.arange(NL, dtype=jnp.int32), jnp.array(turned(NL, FL), dtype=jnp.int32)
    turn = ((place_here - lines[:, None]) % NL == places[None, :])[None, :, :, None, None]
    second = jnp.sum(jnp.where(turn, second[:, None], 0), axis=2)
    second = jnp.where(core == 0, second, second[:, :, ::-1]).reshape(-1)
    left = rows[:, :BS].reshape(NCG, BS, ROWS, BS).transpose(2, 1, 0, 3).reshape(ROWS, BS, NCG * BS)

    shape = (ROWS * BS, LANES)
    squared, own = call(
        square_kernel, "square", [((NL,) + shape, f32), (shape, f32)], [smem(), vmem(), vmem(), vmem()],
        (first, tile, left, slab),
        [pltpu.VMEM((ROWS * NCG * BS, 2 * LANES), jnp.bfloat16)],
    )
    upper, lower = (
        functools.partial(
            call, functools.partial(right_kernel, start), "right", [((ROWS // 2 * GROUP, 2 * LANES), jnp.bfloat16)],
            [smem(), vmem(), vmem()],
        )
        for start in (0, ROWS // 2)
    )
    mine, upper = lax.optimization_barrier((lax.all_to_all(squared, "depth", 0, 0, axis_index_groups=LINES), upper((second, tile, slab))))
    other = lax.ppermute(mine, "depth", [(n, n ^ 1) for n in range(NCG)])
    lower = lower((second, tile, slab))
    purified = call(cube_kernel, "cube", [(shape, f32)], [vmem()] * 5, (mine, other, own, upper, lower))
    return purified.reshape(ROWS, 1, BS, LANES)


def solution(mesh):
    blocks, pattern = P("grid", "depth", None, None), P("grid", "depth", None)
    return jax.shard_map(
        local, mesh=mesh, in_specs=(blocks, pattern, pattern), out_specs=blocks, check_vma=False
    )
```

```python
import functools

import jax
import jax.numpy as jnp
from jax import lax
from jax.experimental import pallas as pl
from jax.experimental.pallas import tpu as pltpu
from jax.sharding import PartitionSpec as P

BS = 32
ROWS = 4
KF = 4
CB = 48
NCG = 8
LANES = 128
TILE = 40
NZ, NX, NYH, NYL, NL, NC = 3, 4, 4, 2, 4, 2
NY = NYH * NYL
FZ, FX, FY, FL = 2, 3, 3, 2


def turned(count, first):
    return [(n + first) % count for n in range(count)]


def device(zh, x, yh, yl):
    return ((zh * NX + x) * NYH + yh) * NYL + yl


FIRST = [
    [device(zh, x, yh, yl) for zh in turned(NZ, FZ) for yh in turned(NYH, FY)]
    for x in range(NX) for yl in range(NYL)
]
SECOND = [
    [device(zh, x, yh, yl) for x in turned(NX, FX) for yl in turned(NYL, 1)]
    for zh in range(NZ) for yh in range(NYH)
]
LINES = [[zl * NC + c for zl in turned(NL, FL)] for c in range(NC)]
PAIRS = [[zl * NC + c for c in range(NC)] for zl in range(NL)]
NP, NS = NZ * NYH, NX * NYL
PIECE = NP * BS + 16
GROUP = NCG * KF * BS


def place(slab, codes, wanted):
    lane_slot = lax.broadcasted_iota(jnp.int32, (8, LANES), 1) // BS
    blocks, columns = [], []
    for code in codes:
        keep = lane_slot == (code & 3)
        block = slab[pl.ds(pl.multiple_of(code >> 14, 8), BS), :].reshape(BS // 8, 8, LANES)
        column = jnp.broadcast_to(slab[pl.ds((code >> 2) & 4095, 1), :], (8, LANES))
        blocks.append(jnp.where(keep, block, 0.0))
        columns.append(jnp.where(keep, column, 0.0)[None])
    every = jnp.concatenate(blocks + columns).reshape(-1, LANES)
    every = every + pltpu.roll(every, 64, 1)
    every = every + pltpu.roll(every, 32, 1)
    count = len(codes)
    blocks = every[: count * BS].reshape(count, BS // 8, 8, LANES)
    columns = every[count * BS :].reshape(count, 8, LANES)
    lands = columns == jnp.stack(wanted)
    return jnp.where(lands[:, None], blocks, 0.0).reshape(count * BS, LANES)


def wanted_of(tile, row):
    return jnp.broadcast_to(tile[BS + 1 + row : BS + 2 + row, :], (8, LANES))


def halves(values, axis):
    high = values.astype(jnp.bfloat16)
    low = (values - high.astype(jnp.float32)).astype(jnp.bfloat16)
    return jnp.concatenate([high, low], axis=axis)


def product(total):
    return (total[:BS, :LANES] + total[:BS, LANES:]) + (total[BS:, :LANES] + total[BS:, LANES:])


def pack_kernel(columns, fill, density, out, copies):
    lane_slot = lax.broadcasted_iota(jnp.int32, (8, LANES), 1) // BS
    line = lax.broadcasted_iota(jnp.int32, (8, LANES), 0)
    numbers = jnp.zeros((8, LANES), jnp.int32)
    for slot in range(ROWS):
        numbers = jnp.where((line == 0) & (lane_slot == slot), columns[0, slot], numbers)
    for row in range(ROWS):
        for slot in range(KF):
            numbers = jnp.where((line == row + 1) & (lane_slot == slot), fill[row, slot], numbers)
    numbers = numbers.astype(jnp.float32)
    data = jnp.concatenate([density[row] for row in range(ROWS)], axis=1)
    out[:BS, :] = data
    out[BS:, :] = numbers
    for n in range(NP):
        copies[n, :BS, 0, :] = data
        copies[n, BS:, 0, :] = numbers[:1]


def spread_kernel(plane, out):
    for member in range(NP):
        block = plane[member, :BS, 0, :]
        column = plane[member, BS:, 0, :]
        for n in range(NS):
            out[n, member * BS : (member + 1) * BS, :] = block
            out[n, NP * BS + member : NP * BS + member + 1, :] = column
    for n in range(NS):
        out[n, NP * BS + NP :, :] = jnp.zeros((PIECE - NP * BS - NP, LANES), jnp.float32)


def square_kernel(codes, tile, left, slab, out, own, right):
    for row in range(0, ROWS, 2):
        wanted = [wanted_of(tile, row)] * NCG + [wanted_of(tile, row + 1)] * NCG
        blocks = place(slab, [codes[row * NCG + t] for t in range(2 * NCG)], wanted)
        right[row * NCG * BS : (row + 2) * NCG * BS, :] = halves(blocks, 1)
    for row in range(ROWS):
        values = right[row * NCG * BS : (row + 1) * NCG * BS, :]
        result = product(jnp.dot(halves(left[row], 0), values, preferred_element_type=jnp.float32))
        rows = slice(row * BS, (row + 1) * BS)
        own[rows, :] = result
        for n in range(NL):
            out[n, rows, :] = result


def right_kernel(start, codes, tile, slab, out):
    batch = 16
    for row in range(ROWS // 2):
        wanted = [wanted_of(tile, start + row)] * batch
        for t in range(row * NCG * KF, (row + 1) * NCG * KF, batch):
            blocks = place(slab, [codes[start * NCG * KF + t + n] for n in range(batch)], wanted)
            out[t * BS : (t + batch) * BS, :] = halves(blocks, 1)


def cube_kernel(mine, other, own, upper, lower, out):
    for row in range(ROWS):
        right = upper if row < ROWS // 2 else lower
        rows = slice(row * BS, (row + 1) * BS)
        total = jnp.zeros((2 * BS, 2 * LANES), jnp.float32)
        for near in range(NL):
            values = jnp.concatenate([mine[near, rows, :], other[near, rows, :]], axis=1)
            start = row % (ROWS // 2) * GROUP + near * NC * LANES
            total = total + jnp.dot(
                halves(values, 0), right[start : start + NC * LANES, :], preferred_element_type=jnp.float32
            )
        out[rows, :] = 3.0 * own[rows, :] - 2.0 * product(total)


def vmem():
    return pl.BlockSpec(memory_space=pltpu.VMEM)


def smem():
    return pl.BlockSpec(memory_space=pltpu.SMEM)


def call(kernel, name, shapes, specs, args, scratch=(), limit=16 * 2**20):
    size = 4 * sum(a.size for a in args)
    shapes = [jax.ShapeDtypeStruct(*shape) for shape in shapes]
    results = pl.pallas_call(
        kernel,
        out_shape=shapes,
        in_specs=specs,
        out_specs=[vmem() for _ in shapes],
        scratch_shapes=list(scratch),
        compiler_params=pltpu.CompilerParams(vmem_limit_bytes=limit),
        cost_estimate=pl.CostEstimate(flops=2**24, bytes_accessed=size, transcendentals=0),
        name=name,
    )(*args)
    return results if len(shapes) > 1 else results[0]


def codes_of(block_row):
    owner, slot = block_row // ROWS, block_row % ROWS
    piece = (owner // NY - FX) % NX * NYL + (owner - 1) % NYL
    member = (owner // (NX * NY) - FZ) % NZ * NYH + (owner % NY // NYL - FY) % NYH
    return (piece * PIECE + member * BS) * 2**14 + (piece * PIECE + NP * BS + member) * 4 + slot


def local(density, columns, fill_columns):
    f32 = jnp.float32
    tile, copies = call(
        pack_kernel, "pack", [((TILE, LANES), f32), ((NP, BS + 1, 1, LANES), f32)], [smem(), smem(), vmem()],
        (columns.reshape(1, ROWS), fill_columns.reshape(ROWS, KF), density.reshape(ROWS, BS, BS)),
        limit=60 * 2**20,
    )
    plane = lax.all_to_all(copies, "grid", 0, 0, axis_index_groups=FIRST)
    pair = lax.all_gather(tile, "depth", axis_index_groups=PAIRS)
    plane, pair = lax.optimization_barrier((plane, pair))
    pieces = call(spread_kernel, "spread", [((NS, PIECE, LANES), f32)], [vmem()], (plane,))
    slab = lax.all_to_all(pieces, "grid", 0, 0, axis_index_groups=SECOND).reshape(NS * PIECE, LANES)

    near = [pair] + [
        lax.ppermute(pair, "depth", [(n, (n + step * NC) % NCG) for n in range(NCG)]) for step in range(1, NL)
    ]
    rows = jnp.stack(near).reshape(NCG, TILE, LANES)
    numbers = rows[:, BS : BS + 5, ::BS].astype(jnp.int32)
    place_here, core = lax.axis_index("depth") // NC, lax.axis_index("depth") % NC
    steps = jnp.arange(NCG, dtype=jnp.int32)
    groups = ((place_here - steps // NC) % NL * NC + steps % NC) * CB
    first = codes_of(numbers[:, 0, :].T + groups[None, :]).reshape(-1)
    second = codes_of(numbers[:, 1:, :].transpose(1, 0, 2) + groups[None, :, None])
    second = second.reshape(ROWS, NL, NC, KF)
    places, lines = jnp.arange(NL, dtype=jnp.int32), jnp.array(turned(NL, FL), dtype=jnp.int32)
    turn = ((place_here - lines[:, None]) % NL == places[None, :])[None, :, :, None, None]
    second = jnp.sum(jnp.where(turn, second[:, None], 0), axis=2)
    second = jnp.where(core == 0, second, second[:, :, ::-1]).reshape(-1)
    left = rows[:, :BS].reshape(NCG, BS, ROWS, BS).transpose(2, 1, 0, 3).reshape(ROWS, BS, NCG * BS)

    shape = (ROWS * BS, LANES)
    squared, own = call(
        square_kernel, "square", [((NL,) + shape, f32), (shape, f32)], [smem(), vmem(), vmem(), vmem()],
        (first, tile, left, slab),
        [pltpu.VMEM((ROWS * NCG * BS, 2 * LANES), jnp.bfloat16)],
    )
    upper, lower = (
        functools.partial(
            call, functools.partial(right_kernel, start), "right", [((ROWS // 2 * GROUP, 2 * LANES), jnp.bfloat16)],
            [smem(), vmem(), vmem()],
        )
        for start in (0, ROWS // 2)
    )
    mine, upper = lax.optimization_barrier((lax.all_to_all(squared, "depth", 0, 0, axis_index_groups=LINES), upper((second, tile, slab))))
    other = lax.ppermute(mine, "depth", [(n, n ^ 1) for n in range(NCG)])
    lower = lower((second, tile, slab))
    purified = call(cube_kernel, "cube", [(shape, f32)], [vmem()] * 5, (mine, other, own, upper, lower))
    return purified.reshape(ROWS, 1, BS, LANES)


def solution(mesh):
    blocks, pattern = P("grid", "depth", None, None), P("grid", "depth", None)
    return jax.shard_map(
        local, mesh=mesh, in_specs=(blocks, pattern, pattern), out_specs=blocks, check_vma=False
    )
```
